256 devices in a mesh: dp: 2 (over x_lo), mp: 128 (over x_hi, z, y, core).
Axes of the slice: x: 4 (x_hi: 2, x_lo: 2; x = x_hi * 2 + x_lo), y: 4, z: 8, core: 2. Of those that a mesh axis runs over, the one named last changes fastest.
Arguments:
- inputs: bfloat16 [1024, 8192], P('dp', 'mp'), may hold values from -6 to 6
- cotangent: bfloat16 [1024, 8192], P('dp', 'mp'), may hold values from -6 to 6
- up_blocks: bfloat16 [128, 6, 256, 256], P('mp'), may hold values from -0.15625 to 0.15625
- down_blocks: bfloat16 [128, 6, 256, 256], P('mp'), may hold values from -0.078125 to 0.078125
- up_left: bfloat16 [8192, 256], P('mp'), may hold values from -0.0625 to 0.0625
- up_right: bfloat16 [256, 32768], P(None, 'mp'), may hold values from -0.375 to 0.375
- down_left: bfloat16 [32768, 256], P('mp'), may hold values from -0.03125 to 0.03125
- down_right: bfloat16 [256, 8192], P(None, 'mp'), may hold values from -0.375 to 0.375
Outputs:
- outputs: bfloat16 [1024, 8192], P('dp', 'mp')
- grad_inputs: bfloat16 [1024, 8192], P('dp', 'mp')
- grad_up_blocks: bfloat16 [128, 6, 256, 256], P('mp')
- grad_down_blocks: bfloat16 [128, 6, 256, 256], P('mp')
- grad_up_left: bfloat16 [8192, 256], P('mp')
- grad_up_right: bfloat16 [256, 32768], P(None, 'mp')
- grad_down_left: bfloat16 [32768, 256], P('mp')
- grad_down_right: bfloat16 [256, 8192], P(None, 'mp')
The draws below stay inside these ranges and needn't reach their ends.
All inputs are finite; a program needn't handle non-finite values.
Results may differ from the reference program's by a relative error of at most 0.013.
Values may be sent and summed in bfloat16 or wider, within the bound.
No kernel may reach another device: no remote copies, remote signals or barrier semaphores. Data moves between devices by JAX's collectives and lax.ppermute only.
A program may use at most 64 MiB of HBM per device.

```python
import jax
import jax.numpy as jnp
import numpy as np

B = 256
LEVELS = 5
R = 256
D = 8192
F = 32768
TOKENS = 1024


def shard_levels(key, dims, pieces, low, largest):
    gain = 1.0
    for position, parts in pieces:
        draws = jax.random.uniform(jax.random.fold_in(jax.random.fold_in(key, 6), position), (parts,), jnp.float32, low / len(pieces), largest / len(pieces))
        gain = gain * jnp.repeat(jnp.exp(draws), dims[position] // parts).reshape((-1,) + (1,) * (len(dims) - 1 - position))
    return gain


def noise(rng, shape, deviation, most, pieces=(), held_as=jnp.bfloat16):
    result = jax.random.normal(rng, shape, jnp.float32) * deviation
    if len(pieces) > 0:
        result = shard_levels(rng, shape, pieces, -0.22, 0.18) * result
    return jnp.clip(result, min=-most, max=most).astype(held_as)


def setup_inputs(seed: int = 0) -> dict:
    key_of = jax.random.split(jax.random.key(seed), 9)
    return {
        "inputs": noise(key_of[0], (TOKENS, D), 1.0, 6.0, ((0, 2), (1, 128))),
        "cotangent": noise(key_of[1], (TOKENS, D), 1.0, 6.0, ((0, 2), (1, 128))),
        "up_blocks": noise(key_of[2], (F // B, LEVELS + 1, B, B), ((LEVELS + 1) * B) ** -0.5, 0.15625, ((0, 128),)),
        "down_blocks": noise(key_of[3], (F // B, LEVELS + 1, B, B), (4 * (LEVELS + 1) * B) ** -0.5, 0.078125, ((0, 128),)),
        "up_left": noise(key_of[4], (D, R), D ** -0.5, 0.0625, ((0, 128),)),
        "up_right": noise(key_of[5], (R, F), R ** -0.5, 0.375, ((1, 128),)),
        "down_left": noise(key_of[6], (F, R), F ** -0.5, 0.03125, ((0, 128),)),
        "down_right": noise(key_of[7], (R, D), R ** -0.5, 0.375, ((1, 128),)),
    }


def gelu_tanh(values):
    return jax.nn.gelu(values, approximate=True)

def partner_table(member):
    shifts = [0] + [1 << height for height in range(LEVELS)]
    return np.arange(F // B) % (D // B) ^ shifts[member]

def target_table(member):
    shifts = [0] + [1 << height for height in range(LEVELS)]
    return np.arange(D // B) ^ shifts[member]

def to_blocks(matrix):
    row_count = matrix.shape[0]
    return matrix.reshape(row_count, 4, D // B, B // 4).transpose(0, 2, 1, 3).reshape(row_count, D // B, B)

def from_blocks(blocks):
    row_count = blocks.shape[0]
    return blocks.reshape(row_count, D // B, 4, B // 4).transpose(0, 2, 1, 3).reshape(row_count, D)

def collect(terms, member):
    row_count = terms.shape[0]
    summed = terms.reshape(row_count, 4, D // B, B).sum(axis=1)
    return summed[:, target_table(member)]

def reference(inputs, cotangent, up_blocks, down_blocks, up_left, up_right, down_left, down_right):
    row_count = inputs.shape[0]
    hidden_count = F // B
    in_blocks = to_blocks(inputs)
    cot_blocks = to_blocks(cotangent)
    input_rank = jnp.dot(inputs, up_left, preferred_element_type=jnp.float32).astype(jnp.bfloat16)
    preact = jnp.dot(input_rank, up_right, preferred_element_type=jnp.float32).reshape(row_count, hidden_count, B)
    for member in range(LEVELS + 1):
        gathered = in_blocks[:, partner_table(member)].astype(jnp.float32)
        preact = preact + jnp.einsum('tjc,jcd->tjd', gathered, up_blocks[:, member].astype(jnp.float32))
    hidden = gelu_tanh(preact).astype(jnp.bfloat16)
    flat_hidden = hidden.reshape(row_count, F)
    hidden_rank = jnp.dot(flat_hidden, down_left, preferred_element_type=jnp.float32).astype(jnp.bfloat16)
    accumulated = jnp.zeros((row_count, D // B, B), jnp.float32)
    for member in range(LEVELS + 1):
        terms = jnp.einsum('tjc,jcd->tjd', hidden.astype(jnp.float32), down_blocks[:, member].astype(jnp.float32))
        accumulated = accumulated + collect(terms, member)
    outputs = (from_blocks(accumulated) + jnp.dot(hidden_rank, down_right, preferred_element_type=jnp.float32)).astype(jnp.bfloat16)
    cot_rank = jnp.dot(cotangent, down_right.T, preferred_element_type=jnp.float32).astype(jnp.bfloat16)
    grad_hidden = jnp.dot(cot_rank, down_left.T, preferred_element_type=jnp.float32).reshape(row_count, hidden_count, B)
    weight_down = []
    for member in range(LEVELS + 1):
        gathered = cot_blocks[:, partner_table(member)].astype(jnp.float32)
        grad_hidden = grad_hidden + jnp.einsum('tjd,jcd->tjc', gathered, down_blocks[:, member].astype(jnp.float32))
        weight_down.append(jnp.einsum('tjc,tjd->jcd', hidden.astype(jnp.float32), gathered))
    grad_preact = jax.vjp(gelu_tanh, preact)[1](grad_hidden)[0].astype(jnp.bfloat16)
    flat_grad = grad_preact.reshape(row_count, F)
    back_rank = jnp.dot(flat_grad, up_right.T, preferred_element_type=jnp.float32).astype(jnp.bfloat16)
    accumulated = jnp.zeros((row_count, D // B, B), jnp.float32)
    weight_up = []
    for member in range(LEVELS + 1):
        terms = jnp.einsum('tjd,jcd->tjc', grad_preact.astype(jnp.float32), up_blocks[:, member].astype(jnp.float32))
        accumulated = accumulated + collect(terms, member)
        gathered = in_blocks[:, partner_table(member)].astype(jnp.float32)
        weight_up.append(jnp.einsum('tjc,tjd->jcd', gathered, grad_preact.astype(jnp.float32)))
    grad_inputs = (from_blocks(accumulated) + jnp.dot(back_rank, up_left.T, preferred_element_type=jnp.float32)).astype(jnp.bfloat16)
    grad_up_blocks = jnp.stack(weight_up, axis=1).astype(jnp.bfloat16)
    grad_down_blocks = jnp.stack(weight_down, axis=1).astype(jnp.bfloat16)
    grad_up_left = jnp.dot(inputs.T, back_rank, preferred_element_type=jnp.float32).astype(jnp.bfloat16)
    grad_up_right = jnp.dot(input_rank.T, flat_grad, preferred_element_type=jnp.float32).astype(jnp.bfloat16)
    grad_down_left = jnp.dot(flat_hidden.T, cot_rank, preferred_element_type=jnp.float32).astype(jnp.bfloat16)
    grad_down_right = jnp.dot(hidden_rank.T, cotangent, preferred_element_type=jnp.float32).astype(jnp.bfloat16)
    return (outputs, grad_inputs, grad_up_blocks, grad_down_blocks, grad_up_left, grad_up_right, grad_down_left, grad_down_right)
```

```python
from functools import partial

import jax
import jax.numpy as jnp
from jax import lax
from jax.sharding import PartitionSpec as P

BF = jnp.bfloat16
F32 = jnp.float32

Z_NEAR = (7, 2, 1, 4, 3, 6, 5, 0)
Z_FAR = (3, 6, 5, 0, 7, 2, 1, 4)


def by_mask(mask):
    return [(i, i ^ mask) for i in range(128)]


def by_z(table):
    return [(i, (i & 0b1000111) | table[i >> 3 & 7] << 3) for i in range(128)]


def send(value, route):
    return lax.ppermute(value, "mp", route)


def swapped_dp(value):
    return lax.ppermute(value, "dp", [(0, 1), (1, 0)])


def dp_sum(value):
    mine = value.astype(BF)
    return (mine.astype(F32) + swapped_dp(mine).astype(F32)).astype(BF)


def mp_sum(partial_sums):
    index = lax.axis_index("mp")
    core, y0, y1 = index & 1, index >> 1 & 1, index >> 2 & 1
    halving = ((1, core), (2, y0 ^ y1), (6, y1))
    value = partial_sums
    for mask, side in halving:
        half = value.shape[0] // 2
        low, high = value[:half], value[half:]
        keep = jnp.where(side == 0, low, high)
        give = jnp.where(side == 0, high, low)
        value = keep + send(give.astype(BF), by_mask(mask)).astype(F32)
    for route in (by_mask(8), by_z(Z_NEAR), by_z(Z_FAR), by_mask(64)):
        value = value + send(value.astype(BF), route).astype(F32)
    value = value.astype(BF)
    for mask, side in halving[::-1]:
        other = send(value, by_mask(mask))
        value = jnp.where(
            side == 0,
            jnp.concatenate([value, other], axis=0),
            jnp.concatenate([other, value], axis=0),
        )
    return value


def bit_value(which_bit):
    return lax.axis_index("mp") >> which_bit & 1


def assemble(piece):
    joined = piece
    for which_bit in (5, 6):
        partner = send(joined, by_mask(1 << which_bit))
        joined = jnp.where(
            bit_value(which_bit) == 0,
            jnp.concatenate([joined, partner], axis=2),
            jnp.concatenate([partner, joined], axis=2),
        )
    return joined


def reduce_quarters(sums):
    value = sums
    for which_bit in (6, 5):
        half = value.shape[2] // 2
        low, high = value[:, :, :half], value[:, :, half:]
        first = bit_value(which_bit) == 0
        keep = jnp.where(first, low, high)
        give = jnp.where(first, high, low)
        value = keep + send(give.astype(BF), by_mask(1 << which_bit)).astype(F32)
    return value


def mm(a, b, dims):
    return lax.dot_general(a, b, (dims, ((), ())), preferred_element_type=F32)


NN = ((1,), (0,))
NT = ((1,), (1,))
TN = ((0,), (0,))


def shards(inputs, cotangent, up_blocks, down_blocks, up_left, up_right, down_left, down_right):
    up, down = up_blocks[0], down_blocks[0]
    terms = up.shape[0]
    masks = [1 << t for t in range(terms - 1)]
    gelu = partial(jax.nn.gelu, approximate=True)

    first = jnp.concatenate([mm(inputs, up_left, NN), mm(cotangent, down_right, NT)], axis=1)
    ranks = mp_sum(first)
    input_rank, cot_rank = ranks[:, :256], ranks[:, 256:]
    own = assemble(jnp.stack([inputs, cotangent]))
    rows = [own] + [send(own, by_mask(mask)) for mask in masks]

    preact = mm(input_rank, up_right, NN)
    grad_hidden = mm(cot_rank, down_left, NT)
    for t in range(terms):
        preact = preact + mm(rows[t][0], up[t], NN)
        grad_hidden = grad_hidden + mm(rows[t][1], down[t], NT)
    hidden_wide, pull = jax.vjp(gelu, preact)
    hidden = hidden_wide.astype(BF)
    grad_preact = pull(grad_hidden)[0].astype(BF)

    second = jnp.concatenate([mm(hidden, down_left, NN), mm(grad_preact, up_right, NT)], axis=1)
    back = mp_sum(second)
    hidden_rank, back_rank = back[:, :256], back[:, 256:]

    sums = jnp.stack([mm(hidden, down[0], NN), mm(grad_preact, up[0], NT)])
    for t in range(1, terms):
        term = jnp.stack([mm(hidden, down[t], NN).astype(BF), mm(grad_preact, up[t], NT).astype(BF)])
        sums = sums + send(term, by_mask(masks[t - 1])).astype(F32)

    weight_down = [mm(hidden, rows[t][1], TN) for t in range(terms)] + [mm(hidden, cot_rank, TN)]
    weight_up = [mm(rows[t][0], grad_preact, TN) for t in range(terms)] + [mm(input_rank, grad_preact, TN)]
    weights = dp_sum(jnp.stack([w.astype(BF) for w in weight_down + weight_up]))
    grad_down_blocks, grad_down_left = weights[:terms], weights[terms]
    grad_up_blocks, grad_up_right = weights[terms + 1 : 2 * terms + 1], weights[2 * terms + 1]

    mine = reduce_quarters(sums)
    outputs = (mine[0] + mm(hidden_rank, down_right, NN)).astype(BF)
    grad_inputs = (mine[1] + mm(back_rank, up_left, NT)).astype(BF)
    narrow = dp_sum(jnp.stack([mm(inputs, back_rank, TN), mm(cotangent, hidden_rank, TN)]))
    return (
        outputs,
        grad_inputs,
        grad_up_blocks[None],
        grad_down_blocks[None],
        narrow[0],
        grad_up_right,
        grad_down_left,
        narrow[1].T,
    )


def solution(mesh):
    placed = (
        P("dp", "mp"),
        P("dp", "mp"),
        P("mp", None, None, None),
        P("mp", None, None, None),
        P("mp", None),
        P(None, "mp"),
        P("mp", None),
        P(None, "mp"),
    )
    return jax.shard_map(shards, mesh=mesh, in_specs=placed, out_specs=placed, check_vma=False)
```

```python
from functools import partial

import jax
import jax.numpy as jnp
from jax import lax
from jax.sharding import PartitionSpec as P

BF = jnp.bfloat16
F32 = jnp.float32

Z_NEAR = (7, 2, 1, 4, 3, 6, 5, 0)
Z_FAR = (3, 6, 5, 0, 7, 2, 1, 4)
Z_TWO = (6, 3, 0, 5, 2, 7, 4, 1)
Z_THREE = (5, 4, 7, 6, 1, 0, 3, 2)

STEPS_A = ['h:core', 'y:halve', 'a:z1', 'z:all', 'a:x2', 'y:join', 'j:core']
STARTS_A = {'z2a': 2, 'z2b': 2, 'core': 'y2'}
ENDS_A = {'q1': 2, 'z1h': 2, 'q2': 3, 'fx': 5, 'y2': 5, 'y1': 5}
FAR = ('z1',)
FXG = {'fx': ('z1',)}
SPLIT = ('z2',)
NTIE = False
STEPS_C = ['h:core', 'y:halve', 'a:x2', 'a:z1', 'a:zn', 'a:zf', 'y:join', 'j:core']
STARTS_C = {'y1': 0, 'y2': 0, 'd0': 2, 'd1': 'q2'}
ENDS_C = {'core': 1, 'z1': 3, 'z2': 3, 'y2': 6, 'y1': 6, 'd0': 6}
PARTS = 2
WAITS = (1, 1)
DMODE = 'swap'
TERMS_C = {'y1': 0, 'y2': 0}


def by_mask(mask):
    return [(i, i ^ mask) for i in range(128)]


def by_z(table):
    return [(i, (i & 0b1000111) | table[i >> 3 & 7] << 3) for i in range(128)]


ROUTES = {
    "core": by_mask(1),
    "y1": by_mask(2),
    "y2": by_mask(4),
    "y3": by_mask(6),
    "z1": by_mask(8),
    "z2": by_mask(16),
    "z4": by_mask(32),
    "z6": by_mask(48),
    "x2": by_mask(64),
    "zn": by_z(Z_NEAR),
    "zf": by_z(Z_FAR),
    "zp": by_z(Z_TWO),
    "zq": by_z(Z_THREE),
}


def send(value, route):
    return lax.ppermute(value, "mp", ROUTES[route])


def swapped_dp(value):
    return lax.ppermute(value, "dp", [(0, 1), (1, 0)])


def after(value, *others):
    return lax.optimization_barrier((value,) + others)[0]


def bit_value(which_bit):
    return lax.axis_index("mp") >> which_bit & 1


def pick(side, low, high):
    return jnp.where(side == 0, low, high)


class Tree:
    def __init__(self, partial_sums, steps, starts, ends):
        self.value = partial_sums
        self.steps, self.starts, self.ends = steps, starts, ends
        self.ops = {}
        self.got = {}

    def side(self, route):
        return {
            "core": lambda: bit_value(0),
            "y1": lambda: bit_value(1) ^ bit_value(2),
            "y3": lambda: bit_value(2),
            "z1": lambda: bit_value(3) ^ bit_value(4),
            "x2": lambda: bit_value(6),
        }[route]()

    def result(self, name):
        if name not in self.got:
            self.got[name] = self.ops[name]()
        return self.got[name]

    def big(self, name, make, go):
        self.ops[name] = lambda: go(make())

    def tied(self, name, value):
        step = self.starts.get(name)
        if step is None:
            return value
        return after(value, self.result(step) if isinstance(step, str) else self.history[step])

    def direct(self, way, first):
        mine = bit_value(1) + 2 * bit_value(2)
        if way == "halve":
            parts = self.value.reshape((4, -1) + self.value.shape[1:])
            take = lambda k: lax.dynamic_index_in_dim(parts, mine ^ k, 0, False)
            gives = after(tuple(take(k).astype(BF) for k in (1, 3, 2)), *first)
            self.value = take(0)
            for give, route in zip(gives, ("y1", "y3", "y2")):
                self.value = self.value + send(give, route).astype(F32)
        else:
            own = after(self.value.astype(BF), *first)
            got = {1: send(own, "y1"), 3: send(own, "y3"), 2: send(own, "y2")}
            stack = jnp.stack([own, got[1], got[2], got[3]])
            self.value = jnp.concatenate(
                [lax.dynamic_index_in_dim(stack, mine ^ k, 0, False) for k in range(4)], axis=0
            )

    def run(self):
        self.history = {}
        for index, step in enumerate(self.steps):
            kind, route = step.split(":")
            first = [self.result(name) for name, at in self.ends.items() if at == index]
            if kind == "y":
                self.direct(route, first)
            elif kind == "z":
                give = after(self.value.astype(BF), *first)
                got = [send(give, r) for r in (("zn", "zp", "zq") if route == "all" else route.split(","))]
                for one in got:
                    self.value = self.value + one.astype(F32)
            elif kind == "h":
                side = self.side(route)
                half = self.value.shape[0] // 2
                low, high = self.value[:half], self.value[half:]
                give = after(pick(side, high, low).astype(BF), *first)
                self.value = pick(side, low, high) + send(give, route).astype(F32)
            elif kind == "a":
                give = after(self.value.astype(BF), *first)
                self.value = self.value + send(give, route).astype(F32)
            else:
                side = self.side(route)
                mine = self.value.astype(BF)
                other = send(after(mine, *first), route)
                self.value = pick(
                    side,
                    jnp.concatenate([mine, other], axis=0),
                    jnp.concatenate([other, mine], axis=0),
                )
            self.history[index] = self.value[:8, :128]
        return self.value


def mm(a, b, dims):
    return lax.dot_general(a, b, (dims, ((), ())), preferred_element_type=F32)


NN = ((1,), (0,))
NT = ((1,), (1,))
TN = ((0,), (0,))


def joined(which_bit, mine, other):
    return pick(
        bit_value(which_bit),
        jnp.concatenate([mine, other], axis=2),
        jnp.concatenate([other, mine], axis=2),
    )


def shards(inputs, cotangent, up_blocks, down_blocks, up_left, up_right, down_left, down_right):
    up, down = up_blocks[0], down_blocks[0]
    terms = up.shape[0]
    gelu = partial(jax.nn.gelu, approximate=True)
    names = ("core", "y1", "y2", "z1", "z2")

    pair = jnp.stack([inputs, cotangent])
    partial_ranks = jnp.concatenate([mm(inputs, up_left, NN), mm(cotangent, down_right, NT)], axis=1)
    tree = Tree(partial_ranks, STEPS_A, STARTS_A, ENDS_A)
    tree.big("q1", lambda: tree.tied("q1", pair), lambda v: send(v, "z4"))
    half = lambda: joined(5, pair, tree.result("q1"))
    tree.big("q2", lambda: tree.tied("q2", half()), lambda v: send(v, "x2"))
    own = lambda: joined(6, half(), tree.result("q2"))
    for name in names:
        if name in FAR:
            tree.big(name + "h", lambda: half(), lambda v, name=name: send(v, name))
        elif name in SPLIT:
            tree.big(name + "a", lambda name=name: tree.tied(name + "a", own()[0]), lambda v: send(v, "z2"))
            tree.big(name + "b", lambda name=name: tree.tied(name + "b", own()[1]), lambda v: send(v, "z6"))
            tree.ops[name] = lambda name=name: (tree.result(name + "a"), tree.result(name + "b"))
        else:
            tree.big(name, lambda name=name: tree.tied(name, own()), lambda v, name=name: send(v, name))
    for group, members in FXG.items():
        tree.big(
            group,
            lambda g=group, m=members: tree.tied(g, jnp.concatenate([tree.result(n + "h") for n in m])),
            lambda v: send(v, "x2"),
        )
        for i, name in enumerate(members):
            tree.ops[name] = lambda g=group, i=i, name=name: joined(
                6, tree.result(name + "h"), tree.result(g)[2 * i : 2 * i + 2]
            )
    ranks = tree.run()
    rows = [own()] + [tree.result(name) for name in names]
    input_rank, cot_rank = ranks[:, :256], ranks[:, 256:]

    preact = mm(input_rank, up_right, NN)
    grad_hidden = mm(cot_rank, down_left, NT)
    for t in range(terms):
        preact = preact + mm(rows[t][0], up[t], NN)
        grad_hidden = grad_hidden + mm(rows[t][1], down[t], NT)
    hidden_wide, pull = jax.vjp(gelu, preact)
    hidden = hidden_wide.astype(BF)
    grad_preact = pull(grad_hidden)[0].astype(BF)

    partial_back = jnp.concatenate([mm(hidden, down_left, NN), mm(grad_preact, up_right, NT)], axis=1)
    tree = Tree(partial_back, STEPS_C, STARTS_C, ENDS_C)
    pairs = [(hidden, rows[t][1]) for t in range(terms)] + [(hidden, cot_rank)]
    pairs += [(rows[t][0], grad_preact) for t in range(terms)] + [(input_rank, grad_preact)]
    edges = [2 * (terms + 1) * i // PARTS for i in range(PARTS + 1)]
    memo = {}

    def chunk(i):
        if i not in memo:
            found = []
            for left, right in pairs[edges[i] : edges[i + 1]]:
                if WAITS[i] is not None:
                    left, right = after((left, right), tree.history[WAITS[i]])
                found.append(mm(left, right, TN).astype(BF))
            memo[i] = jnp.stack(found)
        return memo[i]

    exchanged = swapped_dp if DMODE == "swap" else lambda v: lax.psum(v, "dp")
    for i in range(PARTS):
        tree.big(f"d{i}", lambda i=i: tree.tied(f"d{i}", chunk(i)), exchanged)

    def term(t):
        step = TERMS_C.get(names[t - 1])
        left, right = (hidden, grad_preact) if step is None else after((hidden, grad_preact), tree.history[step])
        return jnp.stack([mm(left, down[t], NN).astype(BF), mm(right, up[t], NT).astype(BF)])

    for t, name in enumerate(names):
        tree.big(name, lambda t=t, name=name: tree.tied(name, term(t + 1)), lambda v, name=name: send(v, name))

    def quarters(value, which_bit):
        middle = value.shape[2] // 2
        low, high = value[:, :, :middle], value[:, :, middle:]
        first = bit_value(which_bit)
        return pick(first, low, high), pick(first, high, low).astype(BF)

    def sums():
        total = jnp.stack([mm(hidden, down[0], NN), mm(grad_preact, up[0], NT)])
        for name in names:
            total = total + tree.result(name).astype(F32)
        return quarters(total, 6)

    tree.big("q2", lambda: tree.tied("q2", sums()[1]), lambda v: send(v, "x2"))
    halves = lambda: quarters(sums()[0] + tree.result("q2").astype(F32), 5)
    tree.big("q1", lambda: tree.tied("q1", halves()[1]), lambda v: send(v, "z4"))
    back = tree.run()
    mine = halves()[0] + tree.result("q1").astype(F32)
    hidden_rank, back_rank = back[:, :256], back[:, 256:]
    outputs = (mine[0] + mm(hidden_rank, down_right, NN)).astype(BF)
    grad_inputs = (mine[1] + mm(back_rank, up_left, NT)).astype(BF)
    narrow = jnp.stack([mm(inputs, back_rank, TN), mm(cotangent, hidden_rank, TN)]).astype(BF)

    def total(part, other):
        return (part.astype(F32) + other.astype(F32)).astype(BF)

    grads = []
    for i in range(PARTS):
        got = tree.result(f"d{i}")
        grads += list(total(chunk(i), got) if DMODE == "swap" else got)
    narrow = total(narrow, swapped_dp(narrow if DMODE == "psum" and not NTIE else after(narrow, *[tree.result(f"d{i}") for i in range(PARTS)])))
    return (
        outputs,
        grad_inputs,
        jnp.stack(grads[terms + 1 : 2 * terms + 1])[None],
        jnp.stack(grads[:terms])[None],
        narrow[0],
        grads[2 * terms + 1],
        grads[terms],
        narrow[1].T,
    )


def solution(mesh):
    placed = (
        P("dp", "mp"),
        P("dp", "mp"),
        P("mp", None, None, None),
        P("mp", None, None, None),
        P("mp", None),
        P(None, "mp"),
        P("mp", None),
        P(None, "mp"),
    )
    return jax.shard_map(shards, mesh=mesh, in_specs=placed, out_specs=placed, check_vma=False)
```

```python
import jax
import jax.numpy as jnp
from jax import lax
from jax.experimental import pallas as pl
from jax.experimental.pallas import tpu as pltpu
from jax.sharding import PartitionSpec as P

BF = jnp.bfloat16
F32 = jnp.float32

Z_NEAR = (7, 2, 1, 4, 3, 6, 5, 0)
Z_FAR = (3, 6, 5, 0, 7, 2, 1, 4)
Z_TWO = (6, 3, 0, 5, 2, 7, 4, 1)
Z_THREE = (5, 4, 7, 6, 1, 0, 3, 2)

STEPS_A = ['h:core', 'y:halve', 'a:z1', 'a:zn', 'a:zf', 'a:x2', 'y:join', 'j:core']
STARTS_A = {'z2a': 3, 'z2b': 3, 'core': 'y2'}
ENDS_A = {'q1': 2, 'z1h': 2, 'q2': 3, 'fx': 6, 'y2': 6, 'y1': 6}
FAR = ('z1',)
FXG = {'fx': ('z1',)}
SPLIT = ('z2',)
NTIE = False
KSTEPS = 2
STEPS_C = ['h:core', 'y:halve', 'a:x2', 'a:z1', 'a:zn', 'a:zf', 'y:join', 'j:core']
STARTS_C = {'y1': 0, 'y2': 0, 'd0': 2, 'd1': 'q2'}
ENDS_C = {'core': 1, 'z1': 3, 'z2': 3, 'y2': 6, 'y1': 6, 'd0': 6}
EDGES = (0, 7, 14)
WAITS = (1, 1)
DMODE = 'swap'
REAL = ('narrow',)


def by_mask(mask):
    return [(i, i ^ mask) for i in range(128)]


def by_z(table):
    return [(i, (i & 0b1000111) | table[i >> 3 & 7] << 3) for i in range(128)]


ROUTES = {
    "core": by_mask(1),
    "y1": by_mask(2),
    "y2": by_mask(4),
    "y3": by_mask(6),
    "z1": by_mask(8),
    "z2": by_mask(16),
    "z4": by_mask(32),
    "z6": by_mask(48),
    "x2": by_mask(64),
    "zn": by_z(Z_NEAR),
    "zf": by_z(Z_FAR),
    "zp": by_z(Z_TWO),
    "zq": by_z(Z_THREE),
}


def send(value, route):
    return lax.ppermute(value, "mp", ROUTES[route])


def swapped_dp(value):
    return lax.ppermute(value, "dp", [(0, 1), (1, 0)])


def after(value, *others):
    return lax.optimization_barrier((value,) + others)[0]


def bound(value, *others):
    for other in others:
        one = other[(0,) * other.ndim].astype(value.dtype)
        value = value + lax.clamp(jnp.zeros_like(one), one, jnp.zeros_like(one))
    return value


def bit_value(which_bit):
    return lax.axis_index("mp") >> which_bit & 1


def pick(side, low, high):
    return jnp.where(side == 0, low, high)


class Tree:
    def __init__(self, partial_sums, steps, starts, ends):
        self.value = partial_sums
        self.steps, self.starts, self.ends = steps, starts, ends
        self.ops = {}
        self.got = {}

    def side(self, route):
        return {
            "core": lambda: bit_value(0),
            "y1": lambda: bit_value(1) ^ bit_value(2),
            "y3": lambda: bit_value(2),
            "z1": lambda: bit_value(3) ^ bit_value(4),
            "x2": lambda: bit_value(6),
        }[route]()

    def result(self, name):
        if name not in self.got:
            self.got[name] = self.ops[name]()
        return self.got[name]

    def big(self, name, make, go):
        self.ops[name] = lambda: go(make())

    def tied(self, name, value):
        step = self.starts.get(name)
        if step is None:
            return value
        hold = bound if name + "s" in REAL else after
        return hold(value, self.result(step) if isinstance(step, str) else self.history[step])

    def direct(self, way, first):
        mine = bit_value(1) + 2 * bit_value(2)
        if way == "halve":
            quarter = self.value.shape[0] // 4
            parts = [self.value[quarter * k : quarter * (k + 1)] for k in range(4)]
            take = lambda k: lax.select_n(mine ^ k, *parts)
            gives = after(tuple(take(k).astype(BF) for k in (1, 3, 2)), *first)
            self.value = take(0)
            for give, route in zip(gives, ("y1", "y3", "y2")):
                self.value = self.value + send(give, route).astype(F32)
        else:
            own = after(self.value.astype(BF), *first)
            got = {1: send(own, "y1"), 3: send(own, "y3"), 2: send(own, "y2")}
            parts = [own, got[1], got[2], got[3]]
            self.value = jnp.concatenate([lax.select_n(mine ^ k, *parts) for k in range(4)], axis=0)

    def run(self):
        self.history = {}
        for index, step in enumerate(self.steps):
            kind, route = step.split(":")
            first = [self.result(name) for name, at in self.ends.items() if at == index]
            must = [self.result(name) for name, at in self.ends.items() if at == index and name + "e" in REAL]
            if must:
                if isinstance(self.value, tuple):
                    self.value = self.value[0], bound(self.value[1], *must)
                else:
                    self.value = bound(self.value, *must)
            if kind == "y":
                self.direct(route, first)
            elif kind == "z":
                give = after(self.value.astype(BF), *first)
                got = [send(give, r) for r in (("zn", "zp", "zq") if route == "all" else route.split(","))]
                for one in got:
                    self.value = self.value + one.astype(F32)
            elif kind == "h" and isinstance(self.value, tuple):
                keep, give = self.value
                self.value = keep + send(after(give, *first), route).astype(F32)
            elif kind == "h":
                side = self.side(route)
                half = self.value.shape[0] // 2
                low, high = self.value[:half], self.value[half:]
                give = after(pick(side, high, low).astype(BF), *first)
                self.value = pick(side, low, high) + send(give, route).astype(F32)
            elif kind == "a":
                give = after(self.value.astype(BF), *first)
                self.value = self.value + send(give, route).astype(F32)
            else:
                side = self.side(route)
                mine = self.value.astype(BF)
                other = send(after(mine, *first), route)
                self.value = pick(
                    side,
                    jnp.concatenate([mine, other], axis=0),
                    jnp.concatenate([other, mine], axis=0),
                )
            self.history[index] = self.value[:8, :128]
        return self.value


def mm(a, b, dims):
    return lax.dot_general(a, b, (dims, ((), ())), preferred_element_type=F32)


NN = ((1,), (0,))
NT = ((1,), (1,))
TN = ((0,), (0,))


def middle(core_ref, pre_ref, grad_ref, rank_ref, up_ref, down_ref, up_right_ref, down_left_ref, *outs):
    act_ref, give_ref, keep_ref, own_ref = outs[:4]
    width = pre_ref.shape[1]
    v = pre_ref[...] + mm(rank_ref[:, :width], up_right_ref[...], NN)
    g = grad_ref[...] + mm(rank_ref[:, width:], down_left_ref[...], NT)
    scale = 0.7978845608028654
    square = v * v
    t = jnp.tanh(scale * (v + 0.044715 * (square * v)))
    half = 0.5 * (1.0 + t)
    slope = half + 0.5 * v * (1.0 - t * t) * (scale * (1.0 + 3 * 0.044715 * square))
    hidden = (v * half).astype(BF)
    grad = (g * slope).astype(BF)
    act_ref[0] = hidden
    act_ref[1] = grad
    ranks = jnp.concatenate([mm(hidden, down_left_ref[...], NN), mm(grad, up_right_ref[...], NT)], axis=1)
    step = pl.program_id(0)
    steps = pl.num_programs(0)

    @pl.when(step < steps // 2)
    def _():
        give_ref[...] = ranks.astype(BF)

    @pl.when(step >= steps // 2)
    def _():
        keep_ref[...] = ranks

    for t_index, out in enumerate((own_ref,) + outs[4:]):
        out[0] = mm(hidden, down_ref[t_index], NN).astype(out.dtype)
        out[1] = mm(grad, up_ref[t_index], NT).astype(out.dtype)


def between(pre, grad, ranks, up, down, up_right, down_left):
    rows, width = pre.shape
    terms = up.shape[0]
    steps = KSTEPS
    block = rows // steps
    core = (lax.axis_index("mp") & 1).astype(jnp.int32).reshape(1)

    def place(i, core_ref):
        return lax.rem(i + (steps // 2) * (1 - core_ref[0]), steps)

    by_rows = lambda cols: pl.BlockSpec((block, cols), lambda i, c: (place(i, c), 0))
    by_pair = pl.BlockSpec((2, block, width), lambda i, c: (0, place(i, c), 0))
    whole = lambda shape: pl.BlockSpec(shape, lambda i, c: (0,) * len(shape))
    first = pl.BlockSpec((block, 2 * width), lambda i, c: (jnp.minimum(i, steps // 2 - 1), 0))
    second = pl.BlockSpec((block, 2 * width), lambda i, c: (jnp.maximum(i - steps // 2, 0), 0))
    pair = lambda dtype: jax.ShapeDtypeStruct((2, rows, width), dtype)
    ranks_half = lambda dtype: jax.ShapeDtypeStruct((rows // 2, 2 * width), dtype)
    return pl.pallas_call(
        middle,
        grid_spec=pltpu.PrefetchScalarGridSpec(
            num_scalar_prefetch=1,
            grid=(steps,),
            in_specs=[
                by_rows(width),
                by_rows(width),
                by_rows(2 * width),
                whole(up.shape),
                whole(down.shape),
                whole(up_right.shape),
                whole(down_left.shape),
            ],
            out_specs=[by_pair, first, second] + [by_pair] * terms,
        ),
        out_shape=[pair(BF), ranks_half(BF), ranks_half(F32), pair(F32)] + [pair(BF)] * (terms - 1),
        compiler_params=pltpu.CompilerParams(vmem_limit_bytes=24 << 20),
        cost_estimate=pl.CostEstimate(flops=2 * 16 * rows * width * width, bytes_accessed=9 << 20, transcendentals=rows * width),
        name="middle",
    )(core, pre, grad, ranks, up, down, up_right, down_left)


def joined(which_bit, mine, other):
    return pick(
        bit_value(which_bit),
        jnp.concatenate([mine, other], axis=2),
        jnp.concatenate([other, mine], axis=2),
    )


def shards(inputs, cotangent, up_blocks, down_blocks, up_left, up_right, down_left, down_right):
    up, down = up_blocks[0], down_blocks[0]
    terms = up.shape[0]
    names = ("core", "y1", "y2", "z1", "z2")

    pair = jnp.stack([inputs, cotangent])
    partial_ranks = jnp.concatenate([mm(inputs, up_left, NN), mm(cotangent, down_right, NT)], axis=1)
    tree = Tree(partial_ranks, STEPS_A, STARTS_A, ENDS_A)
    tree.big("q1", lambda: tree.tied("q1", pair), lambda v: send(v, "z4"))
    half = lambda: joined(5, pair, tree.result("q1"))
    tree.big("q2", lambda: tree.tied("q2", half()), lambda v: send(v, "x2"))
    own = lambda: joined(6, half(), tree.result("q2"))
    for name in names:
        if name in FAR:
            tree.big(name + "h", lambda: half(), lambda v, name=name: send(v, name))
        elif name in SPLIT:
            tree.big(name + "a", lambda name=name: tree.tied(name + "a", own()[0]), lambda v: send(v, "z2"))
            tree.big(name + "b", lambda name=name: tree.tied(name + "b", own()[1]), lambda v: send(v, "z6"))
            tree.ops[name] = lambda name=name: (tree.result(name + "a"), tree.result(name + "b"))
        else:
            tree.big(name, lambda name=name: tree.tied(name, own()), lambda v, name=name: send(v, name))
    for group, members in FXG.items():
        tree.big(
            group,
            lambda g=group, m=members: tree.tied(g, jnp.concatenate([tree.result(n + "h") for n in m])),
            lambda v: send(v, "x2"),
        )
        for i, name in enumerate(members):
            tree.ops[name] = lambda g=group, i=i, name=name: joined(
                6, tree.result(name + "h"), tree.result(g)[2 * i : 2 * i + 2]
            )
    ranks = tree.run()
    rows = [own()] + [tree.result(name) for name in names]
    input_rank, cot_rank = ranks[:, :256], ranks[:, 256:]

    pre = sum(mm(rows[t][0], up[t], NN) for t in range(terms))
    grad = sum(mm(rows[t][1], down[t], NT) for t in range(terms))
    act, give, keep, own_sum, *sent = between(pre, grad, ranks, up, down, up_right, down_left)
    hidden, grad_preact = act[0], act[1]
    tree = Tree((keep, give), STEPS_C, STARTS_C, ENDS_C)
    pairs = [(hidden, rows[t][1]) for t in range(terms)] + [(hidden, cot_rank)]
    pairs += [(rows[t][0], grad_preact) for t in range(terms)] + [(input_rank, grad_preact)]
    edges = EDGES
    memo = {}

    def chunk(i):
        if i not in memo:
            found = []
            for left, right in pairs[edges[i] : edges[i + 1]]:
                if isinstance(WAITS[i], str):
                    left = bound(left, tree.result(WAITS[i]))
                elif isinstance(WAITS[i], float):
                    left = bound(left, tree.history[int(WAITS[i])])
                elif WAITS[i] is not None:
                    left, right = after((left, right), tree.history[WAITS[i]])
                found.append(mm(left, right, TN).astype(BF))
            memo[i] = jnp.stack(found)
        return memo[i]

    exchanged = swapped_dp if DMODE == "swap" else lambda v: lax.psum(v, "dp")
    for i in range(len(EDGES) - 1):
        tree.big(f"d{i}", lambda i=i: tree.tied(f"d{i}", chunk(i)), exchanged)

    for t, name in enumerate(names):
        tree.big(name, lambda t=t, name=name: tree.tied(name, sent[t]), lambda v, name=name: send(v, name))

    def quarters(value, which_bit):
        middle = value.shape[2] // 2
        low, high = value[:, :, :middle], value[:, :, middle:]
        first = bit_value(which_bit)
        return pick(first, low, high), pick(first, high, low).astype(BF)

    def sums():
        total = own_sum
        for name in names:
            total = total + tree.result(name).astype(F32)
        return quarters(total, 6)

    tree.big("q2", lambda: tree.tied("q2", sums()[1]), lambda v: send(v, "x2"))
    halves = lambda: quarters(sums()[0] + tree.result("q2").astype(F32), 5)
    tree.big("q1", lambda: tree.tied("q1", halves()[1]), lambda v: send(v, "z4"))
    back = tree.run()
    hidden_rank, back_rank = back[:, :256], back[:, 256:]
    narrow = jnp.stack([mm(inputs, back_rank, TN), mm(cotangent, hidden_rank, TN)]).astype(BF)

    def total(part, other):
        return (part.astype(F32) + other.astype(F32)).astype(BF)

    grads = []
    for i in range(len(EDGES) - 1):
        got = tree.result(f"d{i}")
        grads += list(total(chunk(i), got) if DMODE == "swap" else got)
    other = swapped_dp(narrow if DMODE == "psum" and not NTIE else after(narrow, *[tree.result(f"d{i}") for i in range(len(EDGES) - 1)]))
    last = tree.result("q1")
    mine = halves()[0] + (bound(last, other) if "narrow" in REAL else last).astype(F32)
    outputs = (mine[0] + mm(hidden_rank, down_right, NN)).astype(BF)
    grad_inputs = (mine[1] + mm(back_rank, up_left, NT)).astype(BF)
    narrow = total(narrow, other)
    return (
        outputs,
        grad_inputs,
        jnp.stack(grads[terms + 1 : 2 * terms + 1])[None],
        jnp.stack(grads[:terms])[None],
        narrow[0],
        grads[2 * terms + 1],
        grads[terms],
        narrow[1].T,
    )


def solution(mesh):
    placed = (
        P("dp", "mp"),
        P("dp", "mp"),
        P("mp", None, None, None),
        P("mp", None, None, None),
        P("mp", None),
        P(None, "mp"),
        P("mp", None),
        P(None, "mp"),
    )
    return jax.shard_map(shards, mesh=mesh, in_specs=placed, out_specs=placed, check_vma=False)
```

```python
from functools import partial

import jax
import jax.numpy as jnp
from jax import lax
from jax.experimental import pallas as pl
from jax.experimental.pallas import tpu as pltpu
from jax.sharding import PartitionSpec as P

BF = jnp.bfloat16
F32 = jnp.float32

Z_NEAR = (7, 2, 1, 4, 3, 6, 5, 0)
Z_FAR = (3, 6, 5, 0, 7, 2, 1, 4)
Z_TWO = (6, 3, 0, 5, 2, 7, 4, 1)
Z_THREE = (5, 4, 7, 6, 1, 0, 3, 2)

STEPS_A = ['h:core', 'y:halve', 'a:z1', 'a:zn', 'a:zf', 'a:x2', 'y:join', 'j:core']
STARTS_A = {'z2a': 3, 'z2b': 3, 'core': 'y2'}
ENDS_A = {'q1': 2, 'z1h': 2, 'q2': 3, 'fx': 6, 'y2': 6, 'y1': 6}
FAR = ('z1',)
FXG = {'fx': ('z1',)}
SPLIT = ('z2',)
NTIE = False
KSTEPS = 2
LATE = ()
OUTT = False
STEPS_C = ['h:core', 'h:y1', 'h:y3', 'a:x2', 'a:z1', 'a:zn', 'a:zf', 'y:rejoin', 'j:core']
STARTS_C = {'y1': 2, 'y2': 2, 'd1': 3, 'd2': 'q2'}
ENDS_C = {'core': 1, 'z1': 4, 'z2': 7, 'y2': 7, 'y1': 7, 'd0': 3, 'd1': 7}
EDGES = (0, 3, 10, 14)
WAITS = (None, 2, 2)
DMODE = 'swap'
REAL = ('narrow', 'q1s')


def by_mask(mask):
    return [(i, i ^ mask) for i in range(128)]


def by_z(table):
    return [(i, (i & 0b1000111) | table[i >> 3 & 7] << 3) for i in range(128)]


ROUTES = {
    "core": by_mask(1),
    "y1": by_mask(2),
    "y2": by_mask(4),
    "y3": by_mask(6),
    "z1": by_mask(8),
    "z2": by_mask(16),
    "z4": by_mask(32),
    "z6": by_mask(48),
    "x2": by_mask(64),
    "zn": by_z(Z_NEAR),
    "zf": by_z(Z_FAR),
    "zp": by_z(Z_TWO),
    "zq": by_z(Z_THREE),
}


def send(value, route):
    return lax.ppermute(value, "mp", ROUTES[route])


def swapped_dp(value):
    return lax.ppermute(value, "dp", [(0, 1), (1, 0)])


def after(value, *others):
    return lax.optimization_barrier((value,) + others)[0]


def bound(value, *others):
    for other in others:
        one = other[(0,) * other.ndim].astype(value.dtype)
        value = value + lax.clamp(jnp.zeros_like(one), one, jnp.zeros_like(one))
    return value


def bit_value(which_bit):
    return lax.axis_index("mp") >> which_bit & 1


def pick(side, low, high):
    return jnp.where(side == 0, low, high)


class Tree:
    def __init__(self, partial_sums, steps, starts, ends):
        self.value = partial_sums
        self.steps, self.starts, self.ends = steps, starts, ends
        self.ops = {}
        self.got = {}

    def side(self, route):
        return {
            "core": lambda: bit_value(0),
            "y1": lambda: bit_value(1) ^ bit_value(2),
            "y3": lambda: bit_value(2),
            "z1": lambda: bit_value(3) ^ bit_value(4),
            "x2": lambda: bit_value(6),
        }[route]()

    def result(self, name):
        if name not in self.got:
            self.got[name] = self.ops[name]()
        return self.got[name]

    def big(self, name, make, go):
        self.ops[name] = lambda: go(make())

    def tied(self, name, value):
        step = self.starts.get(name)
        if step is None:
            return value
        hold = bound if name + "s" in REAL else after
        return hold(value, self.history[step] if step in self.history else self.result(step))

    def direct(self, way, first):
        mine = bit_value(1) + 2 * bit_value(2)
        if way == "halve":
            quarter = self.value.shape[0] // 4
            parts = [self.value[quarter * k : quarter * (k + 1)] for k in range(4)]
            take = lambda k: lax.select_n(mine ^ k, *parts)
            gives = after(tuple(take(k).astype(BF) for k in (1, 3, 2)), *first)
            self.value = take(0)
            for give, route in zip(gives, ("y1", "y3", "y2")):
                self.value = self.value + send(give, route).astype(F32)
        else:
            own = after(self.value.astype(BF), *first)
            got = {1: send(own, "y1"), 3: send(own, "y3"), 2: send(own, "y2")}
            self.history["y2"] = got[2]
            self.history["y3"] = got[3]
            parts = [own, got[1], got[2], got[3]]
            order = (0, 3, 1, 2) if way == "rejoin" else range(4)
            self.value = jnp.concatenate([lax.select_n(mine ^ k, *parts) for k in order], axis=0)

    def run(self):
        self.history = {}
        for index, step in enumerate(self.steps):
            kind, route = step.split(":")
            first = [self.result(name) for name, at in self.ends.items() if at == index]
            must = [self.result(name) for name, at in self.ends.items() if at == index and name + "e" in REAL]
            if must:
                if isinstance(self.value, tuple):
                    self.value = self.value[0], bound(self.value[1], *must)
                else:
                    self.value = bound(self.value, *must)
            if kind == "y":
                self.direct(route, first)
            elif kind == "z":
                give = after(self.value.astype(BF), *first)
                got = [send(give, r) for r in (("zn", "zp", "zq") if route == "all" else route.split(","))]
                for one in got:
                    self.value = self.value + one.astype(F32)
            elif kind == "h" and isinstance(self.value, tuple):
                keep, give = self.value
                self.value = keep + send(after(give, *first), route).astype(F32)
            elif kind == "h":
                side = self.side(route)
                half = self.value.shape[0] // 2
                low, high = self.value[:half], self.value[half:]
                give = after(pick(side, high, low).astype(BF), *first)
                self.value = pick(side, low, high) + send(give, route).astype(F32)
            elif kind == "a":
                give = after(self.value.astype(BF), *first)
                self.value = self.value + send(give, route).astype(F32)
            else:
                side = self.side(route)
                mine = self.value.astype(BF)
                other = send(after(mine, *first), route)
                self.value = pick(
                    side,
                    jnp.concatenate([mine, other], axis=0),
                    jnp.concatenate([other, mine], axis=0),
                )
            self.history[index] = self.value[:8, :128]
        return self.value


def mm(a, b, dims):
    return lax.dot_general(a, b, (dims, ((), ())), preferred_element_type=F32)


NN = ((1,), (0,))
NT = ((1,), (1,))
TN = ((0,), (0,))


def middle(late, core_ref, pre_ref, grad_ref, rank_ref, up_ref, down_ref, up_right_ref, down_left_ref, *outs):
    rows_refs, outs = outs[: 2 * len(late)], outs[2 * len(late) :]
    act_ref, give_ref, keep_ref, own_ref = outs[:4]
    width = pre_ref.shape[1]
    v = pre_ref[...] + mm(rank_ref[:, :width], up_right_ref[...], NN)
    g = grad_ref[...] + mm(rank_ref[:, width:], down_left_ref[...], NT)
    for i, term in enumerate(late):
        v = v + mm(rows_refs[2 * i][...], up_ref[term], NN)
        g = g + mm(rows_refs[2 * i + 1][...], down_ref[term], NT)
    scale = 0.7978845608028654
    square = v * v
    t = jnp.tanh(scale * (v + 0.044715 * (square * v)))
    half = 0.5 * (1.0 + t)
    slope = half + 0.5 * v * (1.0 - t * t) * (scale * (1.0 + 3 * 0.044715 * square))
    hidden = (v * half).astype(BF)
    grad = (g * slope).astype(BF)
    act_ref[0] = hidden
    act_ref[1] = grad
    ranks = jnp.concatenate([mm(hidden, down_left_ref[...], NN), mm(grad, up_right_ref[...], NT)], axis=1)
    step = pl.program_id(0)
    steps = pl.num_programs(0)

    @pl.when(step < steps // 2)
    def _():
        give_ref[...] = ranks.astype(BF)

    @pl.when(step >= steps // 2)
    def _():
        keep_ref[...] = ranks

    for t_index, out in enumerate((own_ref,) + outs[4:]):
        out[0] = mm(hidden, down_ref[t_index], NN).astype(out.dtype)
        out[1] = mm(grad, up_ref[t_index], NT).astype(out.dtype)


def between(pre, grad, ranks, up, down, up_right, down_left, late):
    rows, width = pre.shape
    terms = up.shape[0]
    steps = KSTEPS
    block = rows // steps
    core = (lax.axis_index("mp") & 1).astype(jnp.int32).reshape(1)

    def place(i, core_ref):
        return lax.rem(i + (steps // 2) * (1 - core_ref[0]), steps)

    by_rows = lambda cols: pl.BlockSpec((block, cols), lambda i, c: (place(i, c), 0))
    by_pair = pl.BlockSpec((2, block, width), lambda i, c: (0, place(i, c), 0))
    whole = lambda shape: pl.BlockSpec(shape, lambda i, c: (0,) * len(shape))
    first = pl.BlockSpec((block, 2 * width), lambda i, c: (jnp.minimum(i, steps // 2 - 1), 0))
    second = pl.BlockSpec((block, 2 * width), lambda i, c: (jnp.maximum(i - steps // 2, 0), 0))
    pair = lambda dtype: jax.ShapeDtypeStruct((2, rows, width), dtype)
    ranks_half = lambda dtype: jax.ShapeDtypeStruct((rows // 2, 2 * width), dtype)
    return pl.pallas_call(
        partial(middle, tuple(late)),
        grid_spec=pltpu.PrefetchScalarGridSpec(
            num_scalar_prefetch=1,
            grid=(steps,),
            in_specs=[
                by_rows(width),
                by_rows(width),
                by_rows(2 * width),
                whole(up.shape),
                whole(down.shape),
                whole(up_right.shape),
                whole(down_left.shape),
            ]
            + [by_rows(width)] * (2 * len(late)),
            out_specs=[by_pair, first, second] + [by_pair] * terms,
        ),
        out_shape=[pair(BF), ranks_half(BF), ranks_half(F32), pair(F32)] + [pair(BF)] * (terms - 1),
        compiler_params=pltpu.CompilerParams(vmem_limit_bytes=24 << 20),
        cost_estimate=pl.CostEstimate(flops=2 * 16 * rows * width * width, bytes_accessed=9 << 20, transcendentals=rows * width),
        name="middle",
    )(core, pre, grad, ranks, up, down, up_right, down_left, *[one for pair in late.values() for one in pair])


def joined(which_bit, mine, other):
    return pick(
        bit_value(which_bit),
        jnp.concatenate([mine, other], axis=2),
        jnp.concatenate([other, mine], axis=2),
    )


def shards(inputs, cotangent, up_blocks, down_blocks, up_left, up_right, down_left, down_right):
    up, down = up_blocks[0], down_blocks[0]
    terms = up.shape[0]
    names = ("core", "y1", "y2", "z1", "z2")

    pair = jnp.stack([inputs, cotangent])
    partial_ranks = jnp.concatenate([mm(inputs, up_left, NN), mm(cotangent, down_right, NT)], axis=1)
    tree = Tree(partial_ranks, STEPS_A, STARTS_A, ENDS_A)
    tree.big("q1", lambda: tree.tied("q1", pair), lambda v: send(v, "z4"))
    half = lambda: joined(5, pair, tree.result("q1"))
    tree.big("q2", lambda: tree.tied("q2", half()), lambda v: send(v, "x2"))
    own = lambda: joined(6, half(), tree.result("q2"))
    for name in names:
        if name in FAR:
            tree.big(name + "h", lambda: half(), lambda v, name=name: send(v, name))
        elif name in SPLIT:
            tree.big(name + "a", lambda name=name: tree.tied(name + "a", own()[0]), lambda v: send(v, "z2"))
            tree.big(name + "b", lambda name=name: tree.tied(name + "b", own()[1]), lambda v: send(v, "z6"))
            tree.ops[name] = lambda name=name: (tree.result(name + "a"), tree.result(name + "b"))
        else:
            tree.big(name, lambda name=name: tree.tied(name, own()), lambda v, name=name: send(v, name))
    for group, members in FXG.items():
        tree.big(
            group,
            lambda g=group, m=members: tree.tied(g, jnp.concatenate([tree.result(n + "h") for n in m])),
            lambda v: send(v, "x2"),
        )
        for i, name in enumerate(members):
            tree.ops[name] = lambda g=group, i=i, name=name: joined(
                6, tree.result(name + "h"), tree.result(g)[2 * i : 2 * i + 2]
            )
    ranks = tree.run()
    rows = [own()] + [tree.result(name) for name in names]
    input_rank, cot_rank = ranks[:, :256], ranks[:, 256:]

    late = {t: (rows[t][0], rows[t][1]) for t in LATE}
    pre = sum(mm(rows[t][0], up[t], NN) for t in range(terms) if t not in late)
    grad = sum(mm(rows[t][1], down[t], NT) for t in range(terms) if t not in late)
    act, give, keep, own_sum, *sent = between(pre, grad, ranks, up, down, up_right, down_left, late)
    hidden, grad_preact = act[0], act[1]
    tree = Tree((keep, give), STEPS_C, STARTS_C, ENDS_C)
    pairs = [(hidden, rows[t][1]) for t in range(terms)] + [(hidden, cot_rank)]
    pairs += [(rows[t][0], grad_preact) for t in range(terms)] + [(input_rank, grad_preact)]
    edges = EDGES
    memo = {}

    def chunk(i):
        if i not in memo:
            found = []
            for left, right in pairs[edges[i] : edges[i + 1]]:
                if isinstance(WAITS[i], str):
                    left = bound(left, tree.result(WAITS[i]))
                elif isinstance(WAITS[i], float):
                    left = bound(left, tree.history[int(WAITS[i])])
                elif WAITS[i] is not None:
                    left, right = after((left, right), tree.history[WAITS[i]])
                found.append(mm(left, right, TN).astype(BF))
            memo[i] = jnp.stack(found)
        return memo[i]

    exchanged = swapped_dp if DMODE == "swap" else lambda v: lax.psum(v, "dp")
    for i in range(len(EDGES) - 1):
        tree.big(f"d{i}", lambda i=i: tree.tied(f"d{i}", chunk(i)), exchanged)

    for t, name in enumerate(names):
        tree.big(name, lambda t=t, name=name: tree.tied(name, sent[t]), lambda v, name=name: send(v, name))

    def quarters(value, which_bit):
        middle = value.shape[2] // 2
        low, high = value[:, :, :middle], value[:, :, middle:]
        first = bit_value(which_bit)
        return pick(first, low, high), pick(first, high, low).astype(BF)

    def sums():
        total = own_sum
        for name in names:
            total = total + tree.result(name).astype(F32)
        return quarters(total, 6)

    tree.big("q2", lambda: tree.tied("q2", sums()[1]), lambda v: send(v, "x2"))
    halves = lambda: quarters(sums()[0] + tree.result("q2").astype(F32), 5)
    tree.big("q1", lambda: tree.tied("q1", halves()[1]), lambda v: send(v, "z4"))
    back = tree.run()
    hidden_rank, back_rank = back[:, :256], back[:, 256:]
    narrow = jnp.stack([mm(inputs, back_rank, TN), mm(cotangent, hidden_rank, TN)]).astype(BF)

    def total(part, other):
        return (part.astype(F32) + other.astype(F32)).astype(BF)

    grads = []
    for i in range(len(EDGES) - 1):
        got = tree.result(f"d{i}")
        grads += list(total(chunk(i), got) if DMODE == "swap" else got)
    other = swapped_dp(narrow if DMODE == "psum" and not NTIE else after(narrow, *[tree.result(f"d{i}") for i in range(len(EDGES) - 1)]))
    last = tree.result("q1")
    mine = halves()[0] + (bound(last, other) if "narrow" in REAL else last).astype(F32)
    if OUTT:
        outputs = (mine[0].T + mm(down_right, hidden_rank, ((0,), (1,)))).astype(BF).T
        grad_inputs = (mine[1].T + mm(up_left, back_rank, NT)).astype(BF).T
    else:
        outputs = (mine[0] + mm(hidden_rank, down_right, NN)).astype(BF)
        grad_inputs = (mine[1] + mm(back_rank, up_left, NT)).astype(BF)
    narrow = total(narrow, other)
    return (
        outputs,
        grad_inputs,
        jnp.stack(grads[terms + 1 : 2 * terms + 1])[None],
        jnp.stack(grads[:terms])[None],
        narrow[0],
        grads[2 * terms + 1],
        grads[terms],
        narrow[1].T,
    )


def solution(mesh):
    placed = (
        P("dp", "mp"),
        P("dp", "mp"),
        P("mp", None, None, None),
        P("mp", None, None, None),
        P("mp", None),
        P(None, "mp"),
        P("mp", None),
        P(None, "mp"),
    )
    return jax.shard_map(shards, mesh=mesh, in_specs=placed, out_specs=placed, check_vma=False)
```

```python
from functools import partial

import jax
import jax.numpy as jnp
from jax import lax
from jax.experimental import pallas as pl
from jax.experimental.pallas import tpu as pltpu
from jax.sharding import PartitionSpec as P

BF = jnp.bfloat16
F32 = jnp.float32

Z_NEAR = (7, 2, 1, 4, 3, 6, 5, 0)
Z_FAR = (3, 6, 5, 0, 7, 2, 1, 4)
Z_TWO = (6, 3, 0, 5, 2, 7, 4, 1)
Z_THREE = (5, 4, 7, 6, 1, 0, 3, 2)

STEPS_A = ['h:core', 'y:halve', 'a:z1', 'a:zn', 'a:zf', 'a:x2', 'y:join', 'j:core']
STARTS_A = {'z2a': 3, 'z2b': 3, 'core': 'y2'}
ENDS_A = {'q1': 2, 'z1h': 2, 'q2': 3, 'fx': 6, 'y2': 6, 'y1': 6}
FAR = ('z1',)
FXG = {'fx': ('z1',)}
SPLIT = ('z2',)
NTIE = False
KSTEPS = 2
LATE = ()
OUTT = False
STEPS_C = ['h:core', 'h:y1', 'h:y3', 'a:x2', 'a:z1', 'a:zn', 'a:zf', 'y:rejoin', 'j:core']
STARTS_C = {'y1': 2, 'y2': 2, 'd1': 3, 'd2': 'q2'}
ENDS_C = {'core': 1, 'z1': 4, 'z2': 7, 'y2': 7, 'y1': 7, 'd0': 4, 'd1': 7}
EDGES = (0, 4, 10, 14)
WAITS = (None, 2, 2)
DMODE = 'swap'
REAL = ('narrow', 'q1s')


def by_mask(mask):
    return [(i, i ^ mask) for i in range(128)]


def by_z(table):
    return [(i, (i & 0b1000111) | table[i >> 3 & 7] << 3) for i in range(128)]


ROUTES = {
    "core": by_mask(1),
    "y1": by_mask(2),
    "y2": by_mask(4),
    "y3": by_mask(6),
    "z1": by_mask(8),
    "z2": by_mask(16),
    "z4": by_mask(32),
    "z6": by_mask(48),
    "x2": by_mask(64),
    "zn": by_z(Z_NEAR),
    "zf": by_z(Z_FAR),
    "zp": by_z(Z_TWO),
    "zq": by_z(Z_THREE),
}


def send(value, route):
    return lax.ppermute(value, "mp", ROUTES[route])


def swapped_dp(value):
    return lax.ppermute(value, "dp", [(0, 1), (1, 0)])


def after(value, *others):
    return lax.optimization_barrier((value,) + others)[0]


def bound(value, *others):
    for other in others:
        one = other[(0,) * other.ndim].astype(value.dtype)
        value = value + lax.clamp(jnp.zeros_like(one), one, jnp.zeros_like(one))
    return value


def bit_value(which_bit):
    return lax.axis_index("mp") >> which_bit & 1


def pick(side, low, high):
    return jnp.where(side == 0, low, high)


class Tree:
    def __init__(self, partial_sums, steps, starts, ends):
        self.value = partial_sums
        self.steps, self.starts, self.ends = steps, starts, ends
        self.ops = {}
        self.got = {}

    def side(self, route):
        return {
            "core": lambda: bit_value(0),
            "y1": lambda: bit_value(1) ^ bit_value(2),
            "y3": lambda: bit_value(2),
            "z1": lambda: bit_value(3) ^ bit_value(4),
            "x2": lambda: bit_value(6),
        }[route]()

    def result(self, name):
        if name not in self.got:
            self.got[name] = self.ops[name]()
        return self.got[name]

    def big(self, name, make, go):
        self.ops[name] = lambda: go(make())

    def tied(self, name, value):
        step = self.starts.get(name)
        if step is None:
            return value
        hold = bound if name + "s" in REAL else after
        return hold(value, self.history[step] if step in self.history else self.result(step))

    def direct(self, way, first):
        mine = bit_value(1) + 2 * bit_value(2)
        if way == "halve":
            quarter = self.value.shape[0] // 4
            parts = [self.value[quarter * k : quarter * (k + 1)] for k in range(4)]
            take = lambda k: lax.select_n(mine ^ k, *parts)
            gives = after(tuple(take(k).astype(BF) for k in (1, 3, 2)), *first)
            self.value = take(0)
            for give, route in zip(gives, ("y1", "y3", "y2")):
                self.value = self.value + send(give, route).astype(F32)
        else:
            own = after(self.value.astype(BF), *first)
            got = {1: send(own, "y1"), 3: send(own, "y3"), 2: send(own, "y2")}
            self.history["y2"] = got[2]
            self.history["y3"] = got[3]
            parts = [own, got[1], got[2], got[3]]
            order = (0, 3, 1, 2) if way == "rejoin" else range(4)
            self.value = jnp.concatenate([lax.select_n(mine ^ k, *parts) for k in order], axis=0)

    def run(self):
        self.history = {}
        for index, step in enumerate(self.steps):
            kind, route = step.split(":")
            first = [self.result(name) for name, at in self.ends.items() if at == index]
            must = [self.result(name) for name, at in self.ends.items() if at == index and name + "e" in REAL]
            if must:
                if isinstance(self.value, tuple):
                    self.value = self.value[0], bound(self.value[1], *must)
                else:
                    self.value = bound(self.value, *must)
            if kind == "y":
                self.direct(route, first)
            elif kind == "z":
                give = after(self.value.astype(BF), *first)
                got = [send(give, r) for r in (("zn", "zp", "zq") if route == "all" else route.split(","))]
                for one in got:
                    self.value = self.value + one.astype(F32)
            elif kind == "h" and isinstance(self.value, tuple):
                keep, give = self.value
                self.value = keep + send(after(give, *first), route).astype(F32)
            elif kind == "h":
                side = self.side(route)
                half = self.value.shape[0] // 2
                low, high = self.value[:half], self.value[half:]
                give = after(pick(side, high, low).astype(BF), *first)
                self.value = pick(side, low, high) + send(give, route).astype(F32)
            elif kind == "a":
                give = after(self.value.astype(BF), *first)
                self.value = self.value + send(give, route).astype(F32)
            else:
                side = self.side(route)
                mine = self.value.astype(BF)
                other = send(after(mine, *first), route)
                self.value = pick(
                    side,
                    jnp.concatenate([mine, other], axis=0),
                    jnp.concatenate([other, mine], axis=0),
                )
            self.history[index] = self.value[:8, :128]
        return self.value


def mm(a, b, dims):
    return lax.dot_general(a, b, (dims, ((), ())), preferred_element_type=F32)


NN = ((1,), (0,))
NT = ((1,), (1,))
TN = ((0,), (0,))


def middle(late, core_ref, pre_ref, grad_ref, rank_ref, up_ref, down_ref, up_right_ref, down_left_ref, *outs):
    rows_refs, outs = outs[: 2 * len(late)], outs[2 * len(late) :]
    act_ref, give_ref, keep_ref, own_ref = outs[:4]
    width = pre_ref.shape[1]
    v = pre_ref[...] + mm(rank_ref[:, :width], up_right_ref[...], NN)
    g = grad_ref[...] + mm(rank_ref[:, width:], down_left_ref[...], NT)
    for i, term in enumerate(late):
        v = v + mm(rows_refs[2 * i][...], up_ref[term], NN)
        g = g + mm(rows_refs[2 * i + 1][...], down_ref[term], NT)
    scale = 0.7978845608028654
    square = v * v
    t = jnp.tanh(scale * (v + 0.044715 * (square * v)))
    half = 0.5 * (1.0 + t)
    slope = half + 0.5 * v * (1.0 - t * t) * (scale * (1.0 + 3 * 0.044715 * square))
    hidden = (v * half).astype(BF)
    grad = (g * slope).astype(BF)
    act_ref[0] = hidden
    act_ref[1] = grad
    ranks = jnp.concatenate([mm(hidden, down_left_ref[...], NN), mm(grad, up_right_ref[...], NT)], axis=1)
    step = pl.program_id(0)
    steps = pl.num_programs(0)

    @pl.when(step < steps // 2)
    def _():
        give_ref[...] = ranks.astype(BF)

    @pl.when(step >= steps // 2)
    def _():
        keep_ref[...] = ranks

    for t_index, out in enumerate((own_ref,) + outs[4:]):
        out[0] = mm(hidden, down_ref[t_index], NN).astype(out.dtype)
        out[1] = mm(grad, up_ref[t_index], NT).astype(out.dtype)


def between(pre, grad, ranks, up, down, up_right, down_left, late):
    rows, width = pre.shape
    terms = up.shape[0]
    steps = KSTEPS
    block = rows // steps
    core = (lax.axis_index("mp") & 1).astype(jnp.int32).reshape(1)

    def place(i, core_ref):
        return lax.rem(i + (steps // 2) * (1 - core_ref[0]), steps)

    by_rows = lambda cols: pl.BlockSpec((block, cols), lambda i, c: (place(i, c), 0))
    by_pair = pl.BlockSpec((2, block, width), lambda i, c: (0, place(i, c), 0))
    whole = lambda shape: pl.BlockSpec(shape, lambda i, c: (0,) * len(shape))
    first = pl.BlockSpec((block, 2 * width), lambda i, c: (jnp.minimum(i, steps // 2 - 1), 0))
    second = pl.BlockSpec((block, 2 * width), lambda i, c: (jnp.maximum(i - steps // 2, 0), 0))
    pair = lambda dtype: jax.ShapeDtypeStruct((2, rows, width), dtype)
    ranks_half = lambda dtype: jax.ShapeDtypeStruct((rows // 2, 2 * width), dtype)
    return pl.pallas_call(
        partial(middle, tuple(late)),
        grid_spec=pltpu.PrefetchScalarGridSpec(
            num_scalar_prefetch=1,
            grid=(steps,),
            in_specs=[
                by_rows(width),
                by_rows(width),
                by_rows(2 * width),
                whole(up.shape),
                whole(down.shape),
                whole(up_right.shape),
                whole(down_left.shape),
            ]
            + [by_rows(width)] * (2 * len(late)),
            out_specs=[by_pair, first, second] + [by_pair] * terms,
        ),
        out_shape=[pair(BF), ranks_half(BF), ranks_half(F32), pair(F32)] + [pair(BF)] * (terms - 1),
        compiler_params=pltpu.CompilerParams(vmem_limit_bytes=24 << 20),
        cost_estimate=pl.CostEstimate(flops=2 * 16 * rows * width * width, bytes_accessed=9 << 20, transcendentals=rows * width),
        name="middle",
    )(core, pre, grad, ranks, up, down, up_right, down_left, *[one for pair in late.values() for one in pair])


def joined(which_bit, mine, other):
    return pick(
        bit_value(which_bit),
        jnp.concatenate([mine, other], axis=2),
        jnp.concatenate([other, mine], axis=2),
    )


def shards(inputs, cotangent, up_blocks, down_blocks, up_left, up_right, down_left, down_right):
    up, down = up_blocks[0], down_blocks[0]
    terms = up.shape[0]
    names = ("core", "y1", "y2", "z1", "z2")

    pair = jnp.stack([inputs, cotangent])
    partial_ranks = jnp.concatenate([mm(inputs, up_left, NN), mm(cotangent, down_right, NT)], axis=1)
    tree = Tree(partial_ranks, STEPS_A, STARTS_A, ENDS_A)
    tree.big("q1", lambda: tree.tied("q1", pair), lambda v: send(v, "z4"))
    half = lambda: joined(5, pair, tree.result("q1"))
    tree.big("q2", lambda: tree.tied("q2", half()), lambda v: send(v, "x2"))
    own = lambda: joined(6, half(), tree.result("q2"))
    for name in names:
        if name in FAR:
            tree.big(name + "h", lambda: half(), lambda v, name=name: send(v, name))
        elif name in SPLIT:
            tree.big(name + "a", lambda name=name: tree.tied(name + "a", own()[0]), lambda v: send(v, "z2"))
            tree.big(name + "b", lambda name=name: tree.tied(name + "b", own()[1]), lambda v: send(v, "z6"))
            tree.ops[name] = lambda name=name: (tree.result(name + "a"), tree.result(name + "b"))
        else:
            tree.big(name, lambda name=name: tree.tied(name, own()), lambda v, name=name: send(v, name))
    for group, members in FXG.items():
        tree.big(
            group,
            lambda g=group, m=members: tree.tied(g, jnp.concatenate([tree.result(n + "h") for n in m])),
            lambda v: send(v, "x2"),
        )
        for i, name in enumerate(members):
            tree.ops[name] = lambda g=group, i=i, name=name: joined(
                6, tree.result(name + "h"), tree.result(g)[2 * i : 2 * i + 2]
            )
    ranks = tree.run()
    rows = [own()] + [tree.result(name) for name in names]
    input_rank, cot_rank = ranks[:, :256], ranks[:, 256:]

    late = {t: (rows[t][0], rows[t][1]) for t in LATE}
    pre = sum(mm(rows[t][0], up[t], NN) for t in range(terms) if t not in late)
    grad = sum(mm(rows[t][1], down[t], NT) for t in range(terms) if t not in late)
    act, give, keep, own_sum, *sent = between(pre, grad, ranks, up, down, up_right, down_left, late)
    hidden, grad_preact = act[0], act[1]
    tree = Tree((keep, give), STEPS_C, STARTS_C, ENDS_C)
    pairs = [(hidden, rows[t][1]) for t in range(terms)] + [(hidden, cot_rank)]
    pairs += [(rows[t][0], grad_preact) for t in range(terms)] + [(input_rank, grad_preact)]
    edges = EDGES
    memo = {}

    def chunk(i):
        if i not in memo:
            found = []
            for left, right in pairs[edges[i] : edges[i + 1]]:
                if isinstance(WAITS[i], str):
                    left = bound(left, tree.result(WAITS[i]))
                elif isinstance(WAITS[i], float):
                    left = bound(left, tree.history[int(WAITS[i])])
                elif WAITS[i] is not None:
                    left, right = after((left, right), tree.history[WAITS[i]])
                found.append(mm(left, right, TN).astype(BF))
            memo[i] = jnp.stack(found)
        return memo[i]

    exchanged = swapped_dp if DMODE == "swap" else lambda v: lax.psum(v, "dp")
    for i in range(len(EDGES) - 1):
        tree.big(f"d{i}", lambda i=i: tree.tied(f"d{i}", chunk(i)), exchanged)

    for t, name in enumerate(names):
        tree.big(name, lambda t=t, name=name: tree.tied(name, sent[t]), lambda v, name=name: send(v, name))

    def quarters(value, which_bit):
        middle = value.shape[2] // 2
        low, high = value[:, :, :middle], value[:, :, middle:]
        first = bit_value(which_bit)
        return pick(first, low, high), pick(first, high, low).astype(BF)

    def sums():
        total = own_sum
        for name in names:
            total = total + tree.result(name).astype(F32)
        return quarters(total, 6)

    tree.big("q2", lambda: tree.tied("q2", sums()[1]), lambda v: send(v, "x2"))
    halves = lambda: quarters(sums()[0] + tree.result("q2").astype(F32), 5)
    tree.big("q1", lambda: tree.tied("q1", halves()[1]), lambda v: send(v, "z4"))
    back = tree.run()
    hidden_rank, back_rank = back[:, :256], back[:, 256:]
    narrow = jnp.stack([mm(inputs, back_rank, TN), mm(cotangent, hidden_rank, TN)]).astype(BF)

    def total(part, other):
        return (part.astype(F32) + other.astype(F32)).astype(BF)

    grads = []
    for i in range(len(EDGES) - 1):
        got = tree.result(f"d{i}")
        grads += list(total(chunk(i), got) if DMODE == "swap" else got)
    other = swapped_dp(narrow if DMODE == "psum" and not NTIE else after(narrow, *[tree.result(f"d{i}") for i in range(len(EDGES) - 1)]))
    last = tree.result("q1")
    mine = halves()[0] + (bound(last, other) if "narrow" in REAL else last).astype(F32)
    if OUTT:
        outputs = (mine[0].T + mm(down_right, hidden_rank, ((0,), (1,)))).astype(BF).T
        grad_inputs = (mine[1].T + mm(up_left, back_rank, NT)).astype(BF).T
    else:
        outputs = (mine[0] + mm(hidden_rank, down_right, NN)).astype(BF)
        grad_inputs = (mine[1] + mm(back_rank, up_left, NT)).astype(BF)
    narrow = total(narrow, other)
    return (
        outputs,
        grad_inputs,
        jnp.stack(grads[terms + 1 : 2 * terms + 1])[None],
        jnp.stack(grads[:terms])[None],
        narrow[0],
        grads[2 * terms + 1],
        grads[terms],
        narrow[1].T,
    )


def solution(mesh):
    placed = (
        P("dp", "mp"),
        P("dp", "mp"),
        P("mp", None, None, None),
        P("mp", None, None, None),
        P("mp", None),
        P(None, "mp"),
        P("mp", None),
        P(None, "mp"),
    )
    return jax.shard_map(shards, mesh=mesh, in_specs=placed, out_specs=placed, check_vma=False)
```
